32 devices in a mesh: pencil: 2 (over core), gz: 4 (over y, x), coarse: 4 (over z).
Axes of the slice: x: 2, y: 2, z: 4, core: 2. Of those that a mesh axis runs over, the one named last changes fastest.
Arguments:
- right_side: float32 [16, 64, 1024], P('pencil', 'coarse', 'gz'), may hold values from -6 to 6
- conductivity: float32 [16, 64, 1024], P('pencil', 'coarse', 'gz'), may hold values from 0.2 to 5
- guess: float32 [16, 64, 1024], P('pencil', 'coarse', 'gz'), may hold values from -4 to 4
Outputs:
- updated: float32 [16, 64, 1024], P('pencil', 'coarse', 'gz')
- smoothed_residual: float32 [16, 64, 1024], P('pencil', 'coarse', 'gz')
The draws below stay inside these ranges and needn't reach their ends.
All inputs are finite; a program needn't handle non-finite values.
Results may differ from the reference program's by a relative error of at most 0.00002.
Values sent between devices are 32-bit elements; how exact they have to be, the bound alone decides.
A program may use at most 64 MiB of HBM per device.

```python
import math
import jax
import jax.numpy as jnp

KSWEEP = 4
NX = 16
NY = 64
NZ = 1024


def block_levels(rng, dims, pieces, smallest, top_value):
    factor_of = 1.0
    for axis_at, blocks in pieces:
        heights = jax.random.uniform(jax.random.fold_in(jax.random.fold_in(rng, 6), axis_at), (blocks,), jnp.float32, smallest / len(pieces), top_value / len(pieces))
        factor_of = factor_of * jnp.repeat(jnp.exp(heights), dims[axis_at] // blocks).reshape((-1,) + (1,) * (len(dims) - 1 - axis_at))
    return factor_of


def noise(key, shape, deviation, most, split=(), dtype=jnp.bfloat16):
    level = block_levels(key, shape, split, -0.22, 0.18) if split else 1.0
    drawn = jax.random.normal(key, shape, jnp.float32) * deviation * level
    return jnp.minimum(jnp.maximum(drawn, -most), most).astype(dtype)


def setup_inputs(seed: int = 0) -> dict:
    seeds = jax.random.split(jax.random.key(seed), 4)
    right_side = noise(seeds[0], (NX, NY, NZ), 1.0, 6.0, ((0, 2), (1, 4), (2, 4)), jnp.float32)
    conductivity = jnp.clip(jnp.exp(math.log(5.0) - 3.218876 * jax.random.uniform(seeds[1], (NX, NY, NZ), jnp.float32) ** block_levels(seeds[1], (NX, NY, NZ), ((0, 2), (1, 4), (2, 4)), -0.2, 0.2)), 0.2, 5.0)
    guess = noise(seeds[2], (NX, NY, NZ), 0.3, 4.0, ((0, 2), (1, 4), (2, 4)), jnp.float32)
    return {"right_side": right_side, "conductivity": conductivity, "guess": guess}


def face_terms(padded_k, scale):
    k = padded_k[1:-1, 1:-1, 1:-1]
    return [scale * 0.5 * (k + padded_k[:-2, 1:-1, 1:-1]), scale * 0.5 * (k + padded_k[2:, 1:-1, 1:-1]),
            scale * 0.5 * (k + padded_k[1:-1, :-2, 1:-1]), scale * 0.5 * (k + padded_k[1:-1, 2:, 1:-1]),
            scale * 0.5 * (k + padded_k[1:-1, 1:-1, :-2]), scale * 0.5 * (k + padded_k[1:-1, 1:-1, 2:])]


def diagonal_of(terms):
    return terms[0] + terms[1] + terms[2] + terms[3] + terms[4] + terms[5]


def operate(padded_v, terms, diag):
    v = padded_v[1:-1, 1:-1, 1:-1]
    out = diag * v - terms[0] * padded_v[:-2, 1:-1, 1:-1] - terms[1] * padded_v[2:, 1:-1, 1:-1]
    out = out - terms[2] * padded_v[1:-1, :-2, 1:-1] - terms[3] * padded_v[1:-1, 2:, 1:-1]
    return out - terms[4] * padded_v[1:-1, 1:-1, :-2] - terms[5] * padded_v[1:-1, 1:-1, 2:]


def restrict(field):
    a, b, c = field.shape
    return field.reshape(a // 2, 2, b // 2, 2, c // 2, 2).mean(axis=(1, 3, 5))


def reference(right_side, conductivity, guess):
    theta = 1.1
    delta = 0.8
    sigma = theta / delta
    rho0 = 1.0 / sigma
    rho1 = 1.0 / (2.0 * sigma - rho0)
    terms = face_terms(jnp.pad(conductivity, 1), 1.0)
    dfine = diagonal_of(terms)
    r0 = right_side - operate(jnp.pad(guess, 1), terms, dfine)
    d0 = r0 / (theta * dfine)
    r1 = r0 - operate(jnp.pad(d0, 1), terms, dfine)
    d1 = rho1 * rho0 * d0 + (2.0 * rho1 / delta) * r1 / dfine
    smoothed = r1 - operate(jnp.pad(d1, 1), terms, dfine)
    coarse_r = restrict(r0)
    coarse_k = restrict(conductivity)
    cterms = face_terms(jnp.pad(coarse_k, 1), 0.25)
    dcoarse = diagonal_of(cterms)
    correction = 0.8 * coarse_r / dcoarse
    for sweep in range(KSWEEP - 1):
        correction = correction + 0.8 * (coarse_r - operate(jnp.pad(correction, 1), cterms, dcoarse)) / dcoarse
    lifted = jnp.repeat(jnp.repeat(jnp.repeat(correction, 2, axis=0), 2, axis=1), 2, axis=2)
    updated = guess + d0 + d1 + lifted
    return updated, smoothed
```

```python
import functools

import jax
import jax.numpy as jnp
from jax import lax
from jax.experimental import pallas as pl
from jax.experimental.pallas import tpu as pltpu
from jax.sharding import PartitionSpec as P

KSWEEP = 4
MESH = pl.DeviceIdType.MESH
AXES = ("pencil", "coarse", "gz")
LANES = 128

THETA = 1.1
DELTA = 0.8
SIGMA = THETA / DELTA
RHO0 = 1.0 / SIGMA
RHO1 = 1.0 / (2.0 * SIGMA - RHO0)


def back(v, step, axis):
    return pltpu.roll(v, step, axis)


def ahead(v, step, axis):
    return pltpu.roll(v, v.shape[axis] - step, axis)


def local_operate(v, cx, cy, cz, step):
    gx = cx * (v[1:] - v[:-1])
    zero = jnp.zeros_like(v[:1])
    gy = cy * (v - back(v, step, 1))
    gz = cz * (v - back(v, step, 2))
    return (
        (gy - ahead(gy, step, 1))
        + (gz - ahead(gz, step, 2))
        + (jnp.concatenate([zero, gx], 0) - jnp.concatenate([gx, zero], 0))
    )


def with_ends(inner, low, high):
    return jnp.concatenate([inner[:1] + low, inner[1:-1], inner[-1:] + high], 0)


def y_halo(low, high, shape):
    n, y, z = shape
    half = (n, y // 2, z)
    return jnp.concatenate(
        [jnp.broadcast_to(low[:, None, :], half), jnp.broadcast_to(high[:, None, :], half)], 1
    )


def z_halo(low, high, first, shape):
    n, y, z = shape
    out = []
    for i in range(n):
        at = slice(first + i, first + i + 1)
        out.append(
            jnp.concatenate(
                [
                    jnp.broadcast_to(low[:, at], (y, z // 2)),
                    jnp.broadcast_to(high[:, at], (y, z // 2)),
                ],
                1,
            )
        )
    return jnp.stack(out, 0)


def z_pack(fields, side):
    slot = 0
    lane = lax.broadcasted_iota(jnp.int32, (fields[0].shape[1], LANES), 1)
    packed = jnp.zeros(lane.shape, jnp.float32)
    for v in fields:
        tile = v[:, :, :LANES] if side == 0 else v[:, :, v.shape[2] - LANES :]
        for i in range(v.shape[0]):
            shift = (slot + side) % LANES
            moved = pltpu.roll(tile[i], shift, 1) if shift else tile[i]
            packed = jnp.where(lane == slot, moved, packed)
            slot += 1
    return packed


def pair_sums(v, row_even, lane_even):
    n, y, z = v.shape
    s = v.reshape(n // 2, 2, y, z)
    s = s[:, 0] + s[:, 1]
    s = s + jnp.where(row_even, ahead(s, 1, 1), back(s, 1, 1))
    return s + jnp.where(lane_even, ahead(s, 1, 2), back(s, 1, 2))


def kernel(
    sizes, f_hbm, k_hbm, u_hbm, new_hbm, smooth_hbm,
    f_ref, k_ref, u_ref, new_ref, smooth_ref,
    sxa, rxa, sya, rya, sza, rza,
    d_ref, rxf, syf, ryf, szf, rzf,
    e_ref, rxc, syc, ryc, szc, rzc,
    in_sem, out_sem, send_sem, recv_sem,
):
    nx, ny, nz = f_ref.shape
    hx = nx // 2
    sweeps = KSWEEP - 1
    at = [lax.axis_index(a) for a in AXES]
    has = []
    for dim in range(3):
        has += [at[dim] > 0, at[dim] < sizes[dim] - 1]

    def neighbour(d):
        return {AXES[d // 2]: at[d // 2] + (1 if d % 2 else -1)}

    barrier = pltpu.get_barrier_semaphore()
    for d in range(6):

        @pl.when(has[d])
        def _(d=d):
            pl.semaphore_signal(barrier, inc=1, device_id=neighbour(d), device_id_type=MESH)

    loads = [
        pltpu.make_async_copy(src, dst, in_sem.at[i])
        for i, (src, dst) in enumerate(((k_hbm, k_ref), (u_hbm, u_ref), (f_hbm, f_ref)))
    ]
    for c in loads:
        c.start()

    slots = {}
    slots[0] = [(rxa.at[0], rxa.at[1]), (rya.at[0], rya.at[1]), (rza.at[0], rza.at[1])]
    for j in range(2):
        slots[1 + j] = [(r.at[j, 0], r.at[j, 1]) for r in (rxf, ryf, rzf)]
    for j in range(sweeps):
        slots[3 + j] = [(r.at[j, 0], r.at[j, 1]) for r in (rxc, ryc, rzc)]
    for d in range(6):

        @pl.when(jnp.logical_not(has[d]))
        def _(d=d):
            for part in slots.values():
                ref = part[d // 2][d % 2]
                ref[...] = jnp.zeros(ref.shape, jnp.float32)

    def copy(part, d, src):
        return pltpu.make_async_remote_copy(
            src_ref=src,
            dst_ref=slots[part][d // 2][1 - d % 2],
            send_sem=send_sem.at[part, d],
            recv_sem=recv_sem.at[part, 1 - d % 2 + 2 * (d // 2)],
            device_id=neighbour(d),
            device_id_type=MESH,
        )

    started = []

    def send(part, d, src):
        @pl.when(has[d])
        def _():
            copy(part, d, src).start()

        started.append((part, d, src))

    def receive(part, d, src):
        @pl.when(has[d])
        def _():
            pltpu.make_async_remote_copy(
                src_ref=src,
                dst_ref=slots[part][d // 2][d % 2],
                send_sem=send_sem.at[part, d],
                recv_sem=recv_sem.at[part, d],
                device_id=neighbour(d),
                device_id_type=MESH,
            ).wait_recv()

    lane = lax.broadcasted_iota(jnp.int32, (1, ny, nz), 2)
    row = lax.broadcasted_iota(jnp.int32, (1, ny, nz), 1)
    lane_even, row_even = lane % 2 == 0, row % 2 == 0

    loads[0].wait()
    loads[1].wait()
    k = k_ref[...]
    u = u_ref[...]
    kc = pair_sums(k, row_even, lane_even) * 0.125
    for s in range(2):
        x = -1 if s else 0
        sxa[s, 0] = u[x]
        sxa[s, 1] = k[x]
        sxa[s, 2] = kc[x]
        y = ny - 1 if s else 0
        sya[s, 0:nx] = u_ref[:, y, :]
        sya[s, nx : 2 * nx] = k_ref[:, y, :]
        sya[s, 2 * nx : 2 * nx + hx] = kc[:, y, :]
        sza[s] = z_pack([u, k, kc], s)
    pl.semaphore_wait(barrier, sum(h.astype(jnp.int32) for h in has))
    for d in range(6):
        send(0, d, (sxa, sya, sza)[d // 2].at[d % 2])

    def coefficients(k, step, scale):
        cx = scale * (k[1:] + k[:-1])
        cy = jnp.where(row < step, 0.0, scale * (k + back(k, step, 1)))
        cz = jnp.where(lane < step, 0.0, scale * (k + back(k, step, 2)))
        zero = jnp.zeros_like(k[:1])
        diag = (
            (cy + ahead(cy, step, 1))
            + (cz + ahead(cz, step, 2))
            + (jnp.concatenate([zero, cx], 0) + jnp.concatenate([cx, zero], 0))
        )
        return cx, cy, cz, diag

    def end_coefficients(k, halo, step, scale):
        xl, xh, hy, hz = halo
        bx = scale * (k[:1] + xl), scale * (k[-1:] + xh)
        by = jnp.where((row < step) | (row >= ny - step), scale * (k + hy), 0.0)
        bz = jnp.where((lane < step) | (lane >= nz - step), scale * (k + hz), 0.0)
        return bx, by, bz

    def end_operate(local, v, halo, ends):
        xl, xh, hy, hz = halo
        bx, by, bz = ends
        both = local + by * (v - hy) + bz * (v - hz)
        return with_ends(both, bx[0] * (v[:1] - xl), bx[1] * (v[-1:] - xh))

    cx, cy, cz, diag = coefficients(k, 1, 0.5)
    local_u = local_operate(u, cx, cy, cz, 1)
    ex, ey, ez, ediag = coefficients(kc, 2, 0.125)

    for d in range(6):
        receive(0, d, (sxa, sya, sza)[d // 2].at[d % 2])

    def first_halo(field, n):
        return (
            rxa[0, field][None],
            rxa[1, field][None],
            y_halo(rya[0, field * nx : field * nx + n], rya[1, field * nx : field * nx + n], (n, ny, nz)),
            z_halo(rza[0], rza[1], field * nx, (n, ny, nz)),
        )

    ends = end_coefficients(k, first_halo(1, nx), 1, 0.5)
    diag = with_ends(diag + ends[1] + ends[2], ends[0][0], ends[0][1])
    loads[2].wait()
    r0 = f_ref[...] - end_operate(local_u, u, first_halo(0, nx), ends)

    eends = end_coefficients(kc, first_halo(2, hx), 2, 0.125)
    ediag = with_ends(ediag + eends[1] + eends[2], eends[0][0], eends[0][1])
    einv = 0.8 / ediag
    rc = pair_sums(r0, row_even, lane_even) * 0.125
    ec = rc * einv

    def send_faces(part, v, own, sy, sz, ends):
        own[...] = v
        send(part, 0, own.at[0])
        send(part, 1, own.at[v.shape[0] - 1])
        for s in range(2):
            sy[s] = own[:, ny - 1 if s else 0, :]
            send(part, 2 + s, sy.at[s])
        for s in range(2):
            sz[s] = z_pack([v], s)
            send(part, 4 + s, sz.at[s])

    def halo_of(part, n):
        for d in range(6):
            receive(part, d, slots[part][d // 2][d % 2])
        (xl, xh), (yl, yh), (zl, zh) = slots[part]
        return (
            xl[...][None],
            xh[...][None],
            y_halo(yl[...], yh[...], (n, ny, nz)),
            z_halo(zl[...], zh[...], 0, (n, ny, nz)),
        )

    def send_coarse(j, v):
        send_faces(3 + j, v, e_ref.at[j], syc.at[j], szc.at[j], None)

    def send_fine(j, v):
        send_faces(1 + j, v, d_ref.at[j], syf.at[j], szf.at[j], None)

    def sweep(j, ec, local):
        return ec + (rc - end_operate(local, ec, halo_of(3 + j, hx), eends)) * einv

    send_coarse(0, ec)
    inv = 1.0 / diag
    d0 = r0 * inv * (1.0 / THETA)
    send_fine(0, d0)
    local_e = local_operate(ec, ex, ey, ez, 2)
    local_d0 = local_operate(d0, cx, cy, cz, 1)

    ec = sweep(0, ec, local_e)
    send_coarse(1, ec)
    r1 = r0 - end_operate(local_d0, d0, halo_of(1, nx), ends)
    d1 = (RHO1 * RHO0) * d0 + (2.0 * RHO1 / DELTA) * r1 * inv
    send_fine(1, d1)
    local_e = local_operate(ec, ex, ey, ez, 2)
    local_d1 = local_operate(d1, cx, cy, cz, 1)
    base = u + d0 + d1

    for j in range(1, sweeps - 1):
        ec = sweep(j, ec, local_e)
        send_coarse(j + 1, ec)
        local_e = local_operate(ec, ex, ey, ez, 2)

    smooth_ref[...] = r1 - end_operate(local_d1, d1, halo_of(2, nx), ends)
    out_smooth = pltpu.make_async_copy(smooth_ref, smooth_hbm, out_sem.at[0])
    out_smooth.start()

    ec = sweep(sweeps - 1, ec, local_e)
    new = base.reshape(hx, 2, ny, nz) + ec[:, None]
    new_ref[...] = new.reshape(nx, ny, nz)
    out_new = pltpu.make_async_copy(new_ref, new_hbm, out_sem.at[1])
    out_new.start()

    for part, d, src in started:

        @pl.when(has[d])
        def _(part=part, d=d, src=src):
            copy(part, d, src).wait_send()

    out_smooth.wait()
    out_new.wait()


def on_device(sizes, right_side, conductivity, guess):
    nx, ny, nz = right_side.shape
    hx = nx // 2
    sweeps = KSWEEP - 1
    rows = 2 * nx + hx
    vmem = lambda *shape: pltpu.VMEM(shape, jnp.float32)
    block = jax.ShapeDtypeStruct((nx, ny, nz), jnp.float32)
    anywhere = pl.BlockSpec(memory_space=pl.ANY)
    return pl.pallas_call(
        functools.partial(kernel, sizes),
        out_shape=(block, block),
        in_specs=[anywhere] * 3,
        out_specs=(anywhere, anywhere),
        scratch_shapes=[
            *[vmem(nx, ny, nz)] * 5,
            *[vmem(2, 3, ny, nz)] * 2,
            *[vmem(2, rows, nz)] * 2,
            *[vmem(2, ny, LANES)] * 2,
            vmem(2, nx, ny, nz),
            vmem(2, 2, ny, nz),
            *[vmem(2, 2, nx, nz)] * 2,
            *[vmem(2, 2, ny, LANES)] * 2,
            vmem(sweeps, hx, ny, nz),
            vmem(sweeps, 2, ny, nz),
            *[vmem(sweeps, 2, hx, nz)] * 2,
            *[vmem(sweeps, 2, ny, LANES)] * 2,
            pltpu.SemaphoreType.DMA((3,)),
            pltpu.SemaphoreType.DMA((2,)),
            pltpu.SemaphoreType.DMA((3 + sweeps, 6)),
            pltpu.SemaphoreType.DMA((3 + sweeps, 6)),
        ],
        compiler_params=pltpu.CompilerParams(
            collective_id=0, has_side_effects=True, vmem_limit_bytes=32 * 1024 * 1024
        ),
        cost_estimate=pl.CostEstimate(
            flops=150 * nx * ny * nz, bytes_accessed=20 * nx * ny * nz, transcendentals=0
        ),
    )(right_side, conductivity, guess)


def solution(mesh):
    spec = P("pencil", "coarse", "gz")
    return jax.shard_map(
        functools.partial(on_device, tuple(mesh.shape[a] for a in AXES)),
        mesh=mesh,
        in_specs=(spec, spec, spec),
        out_specs=(spec, spec),
        check_vma=False,
    )
```

```python
import functools

import jax
import jax.numpy as jnp
from jax import lax
from jax.experimental import pallas as pl
from jax.experimental.pallas import tpu as pltpu
from jax.sharding import PartitionSpec as P

KSWEEP = 4
MESH = pl.DeviceIdType.MESH
AXES = ("pencil", "coarse", "gz")
LANES = 128

THETA = 1.1
DELTA = 0.8
SIGMA = THETA / DELTA
RHO0 = 1.0 / SIGMA
RHO1 = 1.0 / (2.0 * SIGMA - RHO0)


def back(v, step, axis):
    return pltpu.roll(v, step, axis)


def ahead(v, step, axis):
    return pltpu.roll(v, v.shape[axis] - step, axis)


def local_operate(v, cx, cy, cz, step):
    gx = cx * (v[1:] - v[:-1])
    zero = jnp.zeros_like(v[:1])
    gy = cy * (v - back(v, step, 1))
    gz = cz * (v - back(v, step, 2))
    return (
        (gy - ahead(gy, step, 1))
        + (gz - ahead(gz, step, 2))
        + (jnp.concatenate([zero, gx], 0) - jnp.concatenate([gx, zero], 0))
    )


def with_ends(inner, low, high):
    return jnp.concatenate([inner[:1] + low, inner[1:-1], inner[-1:] + high], 0)


def pair_sums(v, row_even, lane_even):
    n, y, z = v.shape
    s = v.reshape(n // 2, 2, y, z)
    s = s[:, 0] + s[:, 1]
    s = s + jnp.where(row_even, ahead(s, 1, 1), back(s, 1, 1))
    return s + jnp.where(lane_even, ahead(s, 1, 2), back(s, 1, 2))


def y_halo(low, high, shape):
    n, y, z = shape
    half = (n, y // 2, z)
    return jnp.concatenate(
        [jnp.broadcast_to(low[:, None, :], half), jnp.broadcast_to(high[:, None, :], half)], 1
    )


def z_halo(low, high, first, width, shape):
    n, y, z = shape
    out = []
    for i in range(n):
        a = first + i * width + width - 1
        b = first + i * width
        out.append(
            jnp.concatenate(
                [
                    jnp.broadcast_to(low[:, a : a + 1], (y, z // 2)),
                    jnp.broadcast_to(high[:, b : b + 1], (y, z // 2)),
                ],
                1,
            )
        )
    return jnp.stack(out, 0)


def turned(v, shift):
    shift = shift % v.shape[1]
    return pltpu.roll(v, shift, 1) if shift else v


def z_pack(fields, side):
    at = 0
    lane = lax.broadcasted_iota(jnp.int32, (fields[0][0].shape[1], LANES), 1)
    packed = jnp.zeros(lane.shape, jnp.float32)
    for v, width in fields:
        tile = v[:, :, :LANES] if side == 0 else v[:, :, v.shape[2] - LANES :]
        for i in range(v.shape[0]):
            moved = turned(tile[i], at + (width if side else 0))
            packed = jnp.where((lane >= at) & (lane < at + width), moved, packed)
            at += width
    return packed


def z_unpack(low, high, first, width, n):
    lane = lax.broadcasted_iota(jnp.int32, low.shape, 1)
    out = []
    for i in range(n):
        at = first + i * width
        a = jnp.where(lane < width, turned(high, -at), 0.0)
        out.append(jnp.where(lane >= LANES - width, turned(low, LANES - width - at), a))
    return jnp.stack(out, 0)


def tile_of(rows, shape):
    n, z = shape
    row = lax.broadcasted_iota(jnp.int32, (n, 8, z), 1)
    out = jnp.zeros((n, 8, z), jnp.float32)
    for (a, b), v in rows:
        out = jnp.where((row >= a) & (row < b), jnp.broadcast_to(v[:, None, :], out.shape), out)
    return out


def opposite(d):
    return tuple(-c for c in d)


X_WAYS = ((-1, 0, 0), (1, 0, 0))
Y_WAYS = ((0, -1, 0), (0, 1, 0))
Z_WAYS = ((0, 0, -1), (0, 0, 1))
YZ_WAYS = tuple((0, a, b) for a in (-1, 1) for b in (-1, 1))
AROUND = Y_WAYS + Z_WAYS + YZ_WAYS
FINE, COARSE = 2, KSWEEP - 1


def kernel(
    sizes, f_hbm, k_hbm, u_hbm, new_ref, smooth_ref,
    f_ref, k_ref, u_ref, kc_ref, d_ref, e_ref,
    sxa, rxa, sya, rya, sza, rza, rca,
    syb, ryb, szb, rzb, rcb,
    sxk, rxk, sxd, rxd, sxe, rxe,
    in_sem, send_sem, recv_sem,
):
    nx, ny, nz = f_ref.shape
    hx = nx // 2
    sweeps = KSWEEP - 1
    at = [lax.axis_index(a) for a in AXES]
    side = [{-1: at[i] > 0, 1: at[i] < sizes[i] - 1} for i in range(3)]

    def has(d):
        conditions = [side[i][c] for i, c in enumerate(d) if c]
        return functools.reduce(jnp.logical_and, conditions)

    def neighbour(d):
        return {AXES[i]: at[i] + c for i, c in enumerate(d) if c}

    partners = X_WAYS + AROUND
    barrier = pltpu.get_barrier_semaphore()
    for d in partners:

        @pl.when(has(d))
        def _(d=d):
            pl.semaphore_signal(barrier, inc=1, device_id=neighbour(d), device_id_type=MESH)

    loads = [
        pltpu.make_async_copy(src, dst, in_sem.at[i])
        for i, (src, dst) in enumerate(((k_hbm, k_ref), (u_hbm, u_ref), (f_hbm, f_ref)))
    ]
    for c in loads:
        c.start()

    def x_ways(s, r):
        return {d: (s.at[i], r.at[i]) for i, d in enumerate(X_WAYS)}

    def around(sy, ry, sz, rz, rc):
        out = {d: (sy.at[i], ry.at[i]) for i, d in enumerate(Y_WAYS)}
        out.update({d: (sz.at[i], rz.at[i]) for i, d in enumerate(Z_WAYS)})
        for i, d in enumerate(YZ_WAYS):
            rows = pl.ds(ny - 8 if d[1] > 0 else 0, 8)
            out[d] = (sz.at[1 if d[2] > 0 else 0, rows], rc.at[i])
        return out

    exchanges = {
        "first_x": x_ways(sxa, rxa),
        "first": around(sya, rya, sza, rza, rca),
        "second": around(syb, ryb, szb, rzb, rcb),
        "k": x_ways(sxk, rxk),
    }
    for i in range(2):
        exchanges["d", i] = x_ways(sxd.at[i], rxd.at[i])
    for i in range(sweeps):
        exchanges["e", i] = x_ways(sxe.at[i], rxe.at[i])
    number = {}
    for name, ways in exchanges.items():
        for d in ways:
            number[name, d] = len(number)

    for way in partners:

        @pl.when(jnp.logical_not(has(way)))
        def _(way=way):
            for ways in exchanges.values():
                if way in ways:
                    ref = ways[way][1]
                    ref[...] = jnp.zeros(ref.shape, jnp.float32)

    def copy(name, d):
        return pltpu.make_async_remote_copy(
            src_ref=exchanges[name][d][0],
            dst_ref=exchanges[name][opposite(d)][1],
            send_sem=send_sem.at[number[name, d]],
            recv_sem=recv_sem.at[number[name, opposite(d)]],
            device_id=neighbour(d),
            device_id_type=MESH,
        )

    def send(name):
        for d in exchanges[name]:

            @pl.when(has(d))
            def _(d=d):
                copy(name, d).start()

    def receive(name):
        for d in exchanges[name]:

            @pl.when(has(d))
            def _(d=d):
                pltpu.make_async_remote_copy(
                    src_ref=exchanges[name][d][0],
                    dst_ref=exchanges[name][d][1],
                    send_sem=send_sem.at[number[name, d]],
                    recv_sem=recv_sem.at[number[name, d]],
                    device_id=neighbour(d),
                    device_id_type=MESH,
                ).wait_recv()

    lane = lax.broadcasted_iota(jnp.int32, (1, ny, nz), 2)
    row = lax.broadcasted_iota(jnp.int32, (1, ny, nz), 1)
    lane_even, row_even = lane % 2 == 0, row % 2 == 0

    def put_rows(to, first, ref, depth, step, s):
        n = ref.shape[0]
        for r in range(depth):
            y = ny - 1 - r * step if s else r * step
            to[s, first + r * n : first + (r + 1) * n] = ref[:, y, :]
        return first + depth * n

    loads[0].wait()
    k = k_ref[...]
    kc = pair_sums(k, row_even, lane_even) * 0.125
    kc_ref[...] = kc
    loads[1].wait()
    u = u_ref[...]
    for s in range(2):
        x = -1 if s else 0
        sxa[s, 0] = u[x]
        sxa[s, 1] = k[x]
        sxa[s, 2] = kc[x]
        to = put_rows(sya, 0, u_ref, 1, 1, s)
        to = put_rows(sya, to, k_ref, FINE, 1, s)
        put_rows(sya, to, kc_ref, COARSE, 2, s)
        sza[s] = z_pack([(u, FINE), (k, FINE), (kc, 2 * COARSE)], s)
    pl.semaphore_wait(barrier, sum(has(d).astype(jnp.int32) for d in partners))
    send("first")
    send("first_x")

    def coefficients(k, step, scale, keep):
        cx = scale * (k[1:] + k[:-1])
        cy = scale * (k + back(k, step, 1))
        cz = scale * (k + back(k, step, 2))
        if keep is not None:
            cy = jnp.where(row < keep, 0.0, cy)
            cz = jnp.where(lane < keep, 0.0, cz)
        zero = jnp.zeros_like(k[:1])
        diag = (
            (cy + ahead(cy, step, 1))
            + (cz + ahead(cz, step, 2))
            + (jnp.concatenate([zero, cx], 0) + jnp.concatenate([cx, zero], 0))
        )
        return cx, cy, cz, diag

    def end_coefficients(k, halo, step, scale):
        xl, xh, hy, hz = halo
        bx = scale * (k[:1] + xl), scale * (k[-1:] + xh)
        by = jnp.where((row < step) | (row >= ny - step), scale * (k + hy), 0.0)
        bz = jnp.where((lane < step) | (lane >= nz - step), scale * (k + hz), 0.0)
        return bx, by, bz

    def end_operate(local, v, halo, ends):
        xl, xh, hy, hz = halo
        bx, by, bz = ends
        both = local + by * (v - hy) + bz * (v - hz)
        return with_ends(both, bx[0] * (v[:1] - xl), bx[1] * (v[-1:] - xh))

    cx, cy, cz, diag = coefficients(k, 1, 0.5, 1)
    local_u = local_operate(u, cx, cy, cz, 1)
    _, _, _, ediag = coefficients(kc, 2, 0.125, 2)

    receive("first_x")
    receive("first")

    def first_halo(field, first_row, first_lane, width, n):
        return (
            rxa[0, field][None],
            rxa[1, field][None],
            y_halo(rya[0, first_row : first_row + n], rya[1, first_row : first_row + n], (n, ny, nz)),
            z_halo(rza[0], rza[1], first_lane, width, (n, ny, nz)),
        )

    lane_k, lane_kc = FINE * nx, 2 * FINE * nx
    row_k, row_kc = nx, nx + FINE * nx
    ends = end_coefficients(k, first_halo(1, row_k, lane_k, FINE, nx), 1, 0.5)
    diag = with_ends(diag + ends[1] + ends[2], ends[0][0], ends[0][1])
    loads[2].wait()
    r0 = f_ref[...] - end_operate(local_u, u, first_halo(0, 0, 0, FINE, nx), ends)
    eends = end_coefficients(kc, first_halo(2, row_kc, lane_kc, 2 * COARSE, hx), 2, 0.125)
    ediag = with_ends(ediag + eends[1] + eends[2], eends[0][0], eends[0][1])
    e0 = pair_sums(r0, row_even, lane_even) * 0.125 * (0.8 / ediag)
    d0 = r0 * (1.0 / diag) * (1.0 / THETA)
    d_ref[...] = d0
    e_ref[...] = e0
    for s in range(2):
        to = put_rows(syb, 0, d_ref, FINE, 1, s)
        put_rows(syb, to, e_ref, COARSE, 2, s)
        szb[s] = z_pack([(d0, FINE), (e0, 2 * COARSE)], s)
    send("second")

    def wide_fine(v, ry, first_row, rz, rc, first_lane):
        def rows(i, r):
            return ry[i, first_row + r * nx : first_row + (r + 1) * nx]

        near = [((r, r + 1), rows(1, r)) for r in range(FINE)]
        near += [((7 - r, 8 - r), rows(0, r)) for r in range(FINE)]
        tall = jnp.concatenate([v, tile_of(near, (nx, nz))], 1)
        upper = lax.broadcasted_iota(jnp.int32, (8, LANES), 0) < 4
        ends = []
        for i in range(2):
            corner = jnp.where(upper, rc[2 + i], rc[i])
            ends.append(jnp.concatenate([rz[i], corner], 0))
        return jnp.concatenate([tall, z_unpack(ends[0], ends[1], first_lane, FINE, nx)], 2)

    def wide_coarse(v, ry, first_row, rz, rc, first_lane):
        def rows(i, r):
            return ry[i, first_row + r * hx : first_row + (r + 1) * hx]

        high = tile_of([((2 * r, 2 * r + 2), rows(1, r)) for r in range(COARSE)], (hx, nz))
        low = tile_of([((6 - 2 * r, 8 - 2 * r), rows(0, r)) for r in range(COARSE)], (hx, nz))
        tall = jnp.concatenate([v, high, low], 1)
        ends = [jnp.concatenate([rz[i], rc[2 + i], rc[i]], 0) for i in range(2)]
        return jnp.concatenate([tall, z_unpack(ends[0], ends[1], first_lane, 2 * COARSE, hx)], 2)

    wk = wide_fine(k, rya, row_k, rza, rca, lane_k)
    wkc = wide_coarse(kc, rya, row_kc, rza, rca, lane_kc)
    fine_rows = wk.shape[1]
    for s in range(2):
        x = -1 if s else 0
        sxk[s, :fine_rows] = wk[x]
        sxk[s, fine_rows:] = wkc[x]
    send("k")
    cx, cy, cz, diag = coefficients(wk, 1, 0.5, None)
    ex, ey, ez, ediag = coefficients(wkc, 2, 0.125, None)
    receive("k")
    bx = [0.5 * (wk[x][None] + rxk[s, :fine_rows][None]) for s, x in enumerate((0, -1))]
    be = [0.125 * (wkc[x][None] + rxk[s, fine_rows:][None]) for s, x in enumerate((0, -1))]
    diag = with_ends(diag, bx[0], bx[1])
    ediag = with_ends(ediag, be[0], be[1])
    inv = jnp.where(wk > 0.0, 1.0 / diag, 0.0)
    einv = jnp.where(wkc > 0.0, 0.8 / ediag, 0.0)

    def send_x(name, v):
        for i, d in enumerate(X_WAYS):
            exchanges[name][d][0][...] = v[-1 if i else 0]
        send(name)

    def operate(name, local, v, b):
        receive(name)
        low, high = [exchanges[name][d][1][...][None] for d in X_WAYS]
        return with_ends(local, b[0] * (v[:1] - low), b[1] * (v[-1:] - high))

    receive("second")
    e0 = wide_coarse(e0, ryb, FINE * nx, rzb, rcb, FINE * nx)
    send_x(("e", 0), e0)
    own_d0 = d0
    d0 = wide_fine(d0, ryb, 0, rzb, rcb, 0)
    send_x(("d", 0), d0)
    ec = e0
    local_e = local_operate(ec, ex, ey, ez, 2)
    local_d = local_operate(d0, cx, cy, cz, 1)
    ec = (ec + e0) - einv * operate(("e", 0), local_e, ec, be)
    send_x(("e", 1), ec)
    r1 = THETA * diag * d0 - operate(("d", 0), local_d, d0, bx)
    d1 = (RHO1 * RHO0) * d0 + (2.0 * RHO1 / DELTA) * r1 * inv
    send_x(("d", 1), d1)
    for j in range(1, sweeps):
        local_e = local_operate(ec, ex, ey, ez, 2)
        if j == sweeps - 1:
            local_d = local_operate(d1, cx, cy, cz, 1)
        ec = (ec + e0) - einv * operate(("e", j), local_e, ec, be)
        if j < sweeps - 1:
            send_x(("e", j + 1), ec)
    smooth = r1 - operate(("d", 1), local_d, d1, bx)
    smooth_ref[...] = smooth[:, :ny, :nz]
    base = u + own_d0 + d1[:, :ny, :nz]
    new = base.reshape(hx, 2, ny, nz) + ec[:, :ny, :nz][:, None]
    new_ref[...] = new.reshape(nx, ny, nz)

    for name, ways in exchanges.items():
        for d in ways:

            @pl.when(has(d))
            def _(name=name, d=d):
                copy(name, d).wait_send()


def on_device(sizes, right_side, conductivity, guess):
    nx, ny, nz = right_side.shape
    hx = nx // 2
    sweeps = KSWEEP - 1
    fine = (ny + 8, nz + LANES)
    coarse = (ny + 16, nz + LANES)
    rows_a = nx + FINE * nx + COARSE * hx
    rows_b = FINE * nx + COARSE * hx
    vmem = lambda *shape: pltpu.VMEM(shape, jnp.float32)
    block = jax.ShapeDtypeStruct((nx, ny, nz), jnp.float32)
    anywhere = pl.BlockSpec(memory_space=pl.ANY)
    inside = pl.BlockSpec(memory_space=pltpu.VMEM)
    messages = 2 + 8 + 8 + 2 + 4 + 2 * sweeps
    return pl.pallas_call(
        functools.partial(kernel, sizes),
        out_shape=(block, block),
        in_specs=[anywhere] * 3,
        out_specs=(inside, inside),
        scratch_shapes=[
            *[vmem(nx, ny, nz)] * 3,
            vmem(hx, ny, nz),
            vmem(nx, ny, nz),
            vmem(hx, ny, nz),
            *[vmem(2, 3, ny, nz)] * 2,
            *[vmem(2, rows_a, nz)] * 2,
            *[vmem(2, ny, LANES)] * 2,
            vmem(4, 8, LANES),
            *[vmem(2, rows_b, nz)] * 2,
            *[vmem(2, ny, LANES)] * 2,
            vmem(4, 8, LANES),
            *[vmem(2, fine[0] + coarse[0], fine[1])] * 2,
            *[vmem(2, 2, *fine)] * 2,
            *[vmem(sweeps, 2, *coarse)] * 2,
            pltpu.SemaphoreType.DMA((3,)),
            pltpu.SemaphoreType.DMA((messages,)),
            pltpu.SemaphoreType.DMA((messages,)),
        ],
        compiler_params=pltpu.CompilerParams(
            collective_id=0, has_side_effects=True, vmem_limit_bytes=60 * 1024 * 1024
        ),
        cost_estimate=pl.CostEstimate(
            flops=300 * nx * ny * nz, bytes_accessed=20 * nx * ny * nz, transcendentals=0
        ),
    )(right_side, conductivity, guess)


def solution(mesh):
    spec = P("pencil", "coarse", "gz")
    return jax.shard_map(
        functools.partial(on_device, tuple(mesh.shape[a] for a in AXES)),
        mesh=mesh,
        in_specs=(spec, spec, spec),
        out_specs=(spec, spec),
        check_vma=False,
    )
```

```python
import functools

import jax
import jax.numpy as jnp
from jax import lax
from jax.experimental import pallas as pl
from jax.experimental.pallas import tpu as pltpu
from jax.sharding import PartitionSpec as P

KSWEEP = 4
MESH = pl.DeviceIdType.MESH
AXES = ("pencil", "coarse", "gz")
LANES = 128

THETA = 1.1
DELTA = 0.8
SIGMA = THETA / DELTA
RHO0 = 1.0 / SIGMA
RHO1 = 1.0 / (2.0 * SIGMA - RHO0)


def back(v, step, axis):
    return pltpu.roll(v, step, axis)


def ahead(v, step, axis):
    return pltpu.roll(v, v.shape[axis] - step, axis)


def local_operate(v, cx, cy, cz, step):
    gx = cx * (v[1:] - v[:-1])
    zero = jnp.zeros_like(v[:1])
    gy = cy * (v - back(v, step, 1))
    gz = cz * (v - back(v, step, 2))
    return (
        (gy - ahead(gy, step, 1))
        + (gz - ahead(gz, step, 2))
        + (jnp.concatenate([zero, gx], 0) - jnp.concatenate([gx, zero], 0))
    )


def with_ends(inner, low, high):
    return jnp.concatenate([inner[:1] + low, inner[1:-1], inner[-1:] + high], 0)


def pair_sums(v, row_even, lane_even):
    n, y, z = v.shape
    s = v.reshape(n // 2, 2, y, z)
    s = s[:, 0] + s[:, 1]
    s = s + jnp.where(row_even, ahead(s, 1, 1), back(s, 1, 1))
    return s + jnp.where(lane_even, ahead(s, 1, 2), back(s, 1, 2))


def y_halo(low, high, shape):
    n, y, z = shape
    half = (n, y // 2, z)
    return jnp.concatenate(
        [jnp.broadcast_to(low[:, None, :], half), jnp.broadcast_to(high[:, None, :], half)], 1
    )


def z_halo(low, high, first, width, shape):
    n, y, z = shape
    out = []
    for i in range(n):
        a = first + i * width + width - 1
        b = first + i * width
        out.append(
            jnp.concatenate(
                [
                    jnp.broadcast_to(low[:, a : a + 1], (y, z // 2)),
                    jnp.broadcast_to(high[:, b : b + 1], (y, z // 2)),
                ],
                1,
            )
        )
    return jnp.stack(out, 0)


def turned(v, shift):
    shift = shift % v.shape[1]
    return pltpu.roll(v, shift, 1) if shift else v


def z_pack(fields, side):
    at = 0
    lane = lax.broadcasted_iota(jnp.int32, (fields[0][0].shape[1], LANES), 1)
    packed = jnp.zeros(lane.shape, jnp.float32)
    for v, width in fields:
        tile = v[:, :, :LANES] if side == 0 else v[:, :, v.shape[2] - LANES :]
        for i in range(v.shape[0]):
            moved = turned(tile[i], at + (width if side else 0))
            packed = jnp.where((lane >= at) & (lane < at + width), moved, packed)
            at += width
    return packed


def z_unpack(low, high, first, width, n):
    lane = lax.broadcasted_iota(jnp.int32, low.shape, 1)
    out = []
    for i in range(n):
        at = first + i * width
        a = jnp.where(lane < width, turned(high, -at), 0.0)
        out.append(jnp.where(lane >= LANES - width, turned(low, LANES - width - at), a))
    return jnp.stack(out, 0)


def tile_of(rows, shape):
    n, z = shape
    row = lax.broadcasted_iota(jnp.int32, (n, 8, z), 1)
    out = jnp.zeros((n, 8, z), jnp.float32)
    for (a, b), v in rows:
        out = jnp.where((row >= a) & (row < b), jnp.broadcast_to(v[:, None, :], out.shape), out)
    return out


def opposite(d):
    return tuple(-c for c in d)


X_WAYS = ((-1, 0, 0), (1, 0, 0))
Y_WAYS = ((0, -1, 0), (0, 1, 0))
Z_WAYS = ((0, 0, -1), (0, 0, 1))
YZ_WAYS = tuple((0, a, b) for a in (-1, 1) for b in (-1, 1))
AROUND = Y_WAYS + Z_WAYS + YZ_WAYS
FINE, COARSE = 2, KSWEEP - 1


def kernel(
    sizes, f_hbm, k_hbm, u_hbm, out_ref,
    f_ref, k_ref, u_ref, kc_ref, d_ref, e_ref,
    sxa, rxa, sya, rya, syd, ryd, sza, rza, rca,
    syb, ryb, szb, rzb, rcb,
    sxk, rxk, sxd, rxd, sxe, rxe,
    in_sem, send_sem, recv_sem,
):
    nx, ny, nz = f_ref.shape
    hx = nx // 2
    sweeps = KSWEEP - 1
    at = [lax.axis_index(a) for a in AXES]
    side = [{-1: at[i] > 0, 1: at[i] < sizes[i] - 1} for i in range(3)]

    def has(d):
        conditions = [side[i][c] for i, c in enumerate(d) if c]
        return functools.reduce(jnp.logical_and, conditions)

    def neighbour(d):
        return {AXES[i]: at[i] + c for i, c in enumerate(d) if c}

    partners = X_WAYS + Y_WAYS + Z_WAYS
    barrier = pltpu.get_barrier_semaphore()
    for d in partners:

        @pl.when(has(d))
        def _(d=d):
            pl.semaphore_signal(barrier, inc=1, device_id=neighbour(d), device_id_type=MESH)

    loads = [
        pltpu.make_async_copy(src, dst, in_sem.at[i])
        for i, (src, dst) in enumerate(((k_hbm, k_ref), (u_hbm, u_ref), (f_hbm, f_ref)))
    ]
    for c in loads:
        c.start()

    def x_ways(s, r):
        return {d: (s.at[i], r.at[i]) for i, d in enumerate(X_WAYS)}

    def faces(sy, ry, sz, rz):
        out = {d: (sy.at[i], ry.at[i]) for i, d in enumerate(Y_WAYS)}
        out.update({d: (sz.at[i], rz.at[i]) for i, d in enumerate(Z_WAYS)})
        return out

    def corners(sz, rc):
        out = {}
        for i, d in enumerate(YZ_WAYS):
            rows = pl.ds(ny - 8 if d[1] > 0 else 0, 8)
            out[d] = (sz.at[1 if d[2] > 0 else 0, rows], rc.at[i])
        return out

    exchanges = {
        "first_x": x_ways(sxa, rxa),
        "first": faces(sya, rya, sza, rza),
        "deep": {d: (syd.at[i], ryd.at[i]) for i, d in enumerate(Y_WAYS)},
        "first_corner": corners(sza, rca),
        "second_corner": corners(szb, rcb),
        "second": faces(syb, ryb, szb, rzb),
        "k": x_ways(sxk, rxk),
    }
    for i in range(2):
        exchanges["d", i] = x_ways(sxd.at[i], rxd.at[i])
    for i in range(sweeps):
        exchanges["e", i] = x_ways(sxe.at[i], rxe.at[i])
    number = {}
    for name, ways in exchanges.items():
        for d in ways:
            number[name, d] = len(number)

    for way in X_WAYS + AROUND:

        @pl.when(jnp.logical_not(has(way)))
        def _(way=way):
            for ways in exchanges.values():
                if way in ways:
                    ref = ways[way][1]
                    ref[...] = jnp.zeros(ref.shape, jnp.float32)

    def copy(name, d):
        return pltpu.make_async_remote_copy(
            src_ref=exchanges[name][d][0],
            dst_ref=exchanges[name][opposite(d)][1],
            send_sem=send_sem.at[number[name, d]],
            recv_sem=recv_sem.at[number[name, opposite(d)]],
            device_id=neighbour(d),
            device_id_type=MESH,
        )

    def send(name):
        for d in exchanges[name]:

            @pl.when(has(d))
            def _(d=d):
                copy(name, d).start()

    def receive(name):
        for d in exchanges[name]:

            @pl.when(has(d))
            def _(d=d):
                pltpu.make_async_remote_copy(
                    src_ref=exchanges[name][d][0],
                    dst_ref=exchanges[name][d][1],
                    send_sem=send_sem.at[number[name, d]],
                    recv_sem=recv_sem.at[number[name, d]],
                    device_id=neighbour(d),
                    device_id_type=MESH,
                ).wait_recv()

    lane = lax.broadcasted_iota(jnp.int32, (1, ny, nz), 2)
    row = lax.broadcasted_iota(jnp.int32, (1, ny, nz), 1)
    lane_even, row_even = lane % 2 == 0, row % 2 == 0

    def put_rows(to, first, ref, depths, step, s):
        n = ref.shape[0]
        for r in depths:
            y = ny - 1 - r * step if s else r * step
            to[s, first : first + n] = ref[:, y, :]
            first += n
        return first

    loads[0].wait()
    k = k_ref[...]
    kc = pair_sums(k, row_even, lane_even) * 0.125
    kc_ref[...] = kc
    loads[1].wait()
    u = u_ref[...]
    for s in range(2):
        x = -1 if s else 0
        sxa[s, 0] = u[x]
        sxa[s, 1] = k[x]
        sxa[s, 2] = kc[x]
        to = put_rows(sya, 0, u_ref, (0,), 1, s)
        to = put_rows(sya, to, k_ref, (0,), 1, s)
        put_rows(sya, to, kc_ref, (0,), 2, s)
        to = put_rows(syd, 0, k_ref, range(1, FINE), 1, s)
        put_rows(syd, to, kc_ref, range(1, COARSE), 2, s)
        sza[s] = z_pack([(u, FINE), (k, FINE), (kc, 2 * COARSE)], s)
    pl.semaphore_wait(barrier, sum(has(d).astype(jnp.int32) for d in partners))
    send("first")
    send("first_x")
    send("deep")

    def coefficients(k, step, scale, keep):
        cx = scale * (k[1:] + k[:-1])
        cy = scale * (k + back(k, step, 1))
        cz = scale * (k + back(k, step, 2))
        if keep is not None:
            cy = jnp.where(row < keep, 0.0, cy)
            cz = jnp.where(lane < keep, 0.0, cz)
        zero = jnp.zeros_like(k[:1])
        diag = (
            (cy + ahead(cy, step, 1))
            + (cz + ahead(cz, step, 2))
            + (jnp.concatenate([zero, cx], 0) + jnp.concatenate([cx, zero], 0))
        )
        return cx, cy, cz, diag

    def end_coefficients(k, halo, step, scale):
        xl, xh, hy, hz = halo
        bx = scale * (k[:1] + xl), scale * (k[-1:] + xh)
        by = jnp.where((row < step) | (row >= ny - step), scale * (k + hy), 0.0)
        bz = jnp.where((lane < step) | (lane >= nz - step), scale * (k + hz), 0.0)
        return bx, by, bz

    def end_operate(local, v, halo, ends):
        xl, xh, hy, hz = halo
        bx, by, bz = ends
        both = local + by * (v - hy) + bz * (v - hz)
        return with_ends(both, bx[0] * (v[:1] - xl), bx[1] * (v[-1:] - xh))

    cx, cy, cz, diag = coefficients(k, 1, 0.5, 1)
    local_u = local_operate(u, cx, cy, cz, 1)
    _, _, _, ediag = coefficients(kc, 2, 0.125, 2)

    receive("first_x")
    receive("first")
    send("first_corner")

    def first_halo(field, first_row, first_lane, width, n):
        return (
            rxa[0, field][None],
            rxa[1, field][None],
            y_halo(rya[0, first_row : first_row + n], rya[1, first_row : first_row + n], (n, ny, nz)),
            z_halo(rza[0], rza[1], first_lane, width, (n, ny, nz)),
        )

    lane_k, lane_kc = FINE * nx, 2 * FINE * nx
    row_k, row_kc = nx, 2 * nx
    ends = end_coefficients(k, first_halo(1, row_k, lane_k, FINE, nx), 1, 0.5)
    diag = with_ends(diag + ends[1] + ends[2], ends[0][0], ends[0][1])
    loads[2].wait()
    r0 = f_ref[...] - end_operate(local_u, u, first_halo(0, 0, 0, FINE, nx), ends)
    eends = end_coefficients(kc, first_halo(2, row_kc, lane_kc, 2 * COARSE, hx), 2, 0.125)
    ediag = with_ends(ediag + eends[1] + eends[2], eends[0][0], eends[0][1])
    e0 = pair_sums(r0, row_even, lane_even) * 0.125 * (0.8 / ediag)
    d0 = r0 * (1.0 / diag) * (1.0 / THETA)
    d_ref[...] = d0
    e_ref[...] = e0
    for s in range(2):
        to = put_rows(syb, 0, d_ref, range(FINE), 1, s)
        put_rows(syb, to, e_ref, range(COARSE), 2, s)
        szb[s] = z_pack([(d0, FINE), (e0, 2 * COARSE)], s)
    send("second_corner")
    send("second")

    def wide_fine(v, rows, rz, rc, first_lane):
        near = [((r, r + 1), rows(1, r)) for r in range(FINE)]
        near += [((7 - r, 8 - r), rows(0, r)) for r in range(FINE)]
        tall = jnp.concatenate([v, tile_of(near, (nx, nz))], 1)
        upper = lax.broadcasted_iota(jnp.int32, (8, LANES), 0) < 4
        ends = []
        for i in range(2):
            corner = jnp.where(upper, rc[2 + i], rc[i])
            ends.append(jnp.concatenate([rz[i], corner], 0))
        return jnp.concatenate([tall, z_unpack(ends[0], ends[1], first_lane, FINE, nx)], 2)

    def wide_coarse(v, rows, rz, rc, first_lane):
        high = tile_of([((2 * r, 2 * r + 2), rows(1, r)) for r in range(COARSE)], (hx, nz))
        low = tile_of([((6 - 2 * r, 8 - 2 * r), rows(0, r)) for r in range(COARSE)], (hx, nz))
        tall = jnp.concatenate([v, high, low], 1)
        ends = [jnp.concatenate([rz[i], rc[2 + i], rc[i]], 0) for i in range(2)]
        return jnp.concatenate([tall, z_unpack(ends[0], ends[1], first_lane, 2 * COARSE, hx)], 2)

    def rows_of(ref, first, n):
        return lambda i, r: ref[i, first + r * n : first + (r + 1) * n]

    def first_or_deep(first, deep, n):
        return lambda i, r: (rows_of(ryd, deep, n)(i, r - 1) if r else rows_of(rya, first, n)(i, 0))

    receive("deep")
    receive("first_corner")
    wk = wide_fine(k, first_or_deep(row_k, 0, nx), rza, rca, lane_k)
    wkc = wide_coarse(kc, first_or_deep(row_kc, (FINE - 1) * nx, hx), rza, rca, lane_kc)
    fine_rows = wk.shape[1]
    for s in range(2):
        x = -1 if s else 0
        sxk[s, :fine_rows] = wk[x]
        sxk[s, fine_rows:] = wkc[x]
    send("k")
    cx, cy, cz, diag = coefficients(wk, 1, 0.5, None)
    ex, ey, ez, ediag = coefficients(wkc, 2, 0.125, None)
    receive("k")
    bx = [0.5 * (wk[x][None] + rxk[s, :fine_rows][None]) for s, x in enumerate((0, -1))]
    be = [0.125 * (wkc[x][None] + rxk[s, fine_rows:][None]) for s, x in enumerate((0, -1))]
    diag = with_ends(diag, bx[0], bx[1])
    ediag = with_ends(ediag, be[0], be[1])
    inv = jnp.where(wk > 0.0, 1.0 / diag, 0.0)
    einv = jnp.where(wkc > 0.0, 0.8 / ediag, 0.0)

    def send_x(name, v):
        for i, d in enumerate(X_WAYS):
            exchanges[name][d][0][...] = v[-1 if i else 0]
        send(name)

    def operate(name, local, v, b):
        receive(name)
        low, high = [exchanges[name][d][1][...][None] for d in X_WAYS]
        return with_ends(local, b[0] * (v[:1] - low), b[1] * (v[-1:] - high))

    receive("second")
    receive("second_corner")
    e0 = wide_coarse(e0, rows_of(ryb, FINE * nx, hx), rzb, rcb, FINE * nx)
    send_x(("e", 0), e0)
    own_d0 = d0
    d0 = wide_fine(d0, rows_of(ryb, 0, nx), rzb, rcb, 0)
    send_x(("d", 0), d0)
    ec = e0
    local_e = local_operate(ec, ex, ey, ez, 2)
    local_d = local_operate(d0, cx, cy, cz, 1)
    ec = (ec + e0) - einv * operate(("e", 0), local_e, ec, be)
    send_x(("e", 1), ec)
    r1 = THETA * diag * d0 - operate(("d", 0), local_d, d0, bx)
    d1 = (RHO1 * RHO0) * d0 + (2.0 * RHO1 / DELTA) * r1 * inv
    send_x(("d", 1), d1)
    for j in range(1, sweeps):
        local_e = local_operate(ec, ex, ey, ez, 2)
        if j == sweeps - 1:
            local_d = local_operate(d1, cx, cy, cz, 1)
        ec = (ec + e0) - einv * operate(("e", j), local_e, ec, be)
        if j < sweeps - 1:
            send_x(("e", j + 1), ec)
    smooth = r1 - operate(("d", 1), local_d, d1, bx)
    out_ref[1] = smooth[:, :ny, :nz]
    base = u + own_d0 + d1[:, :ny, :nz]
    new = base.reshape(hx, 2, ny, nz) + ec[:, :ny, :nz][:, None]
    out_ref[0] = new.reshape(nx, ny, nz)

    for name, ways in exchanges.items():
        for d in ways:

            @pl.when(has(d))
            def _(name=name, d=d):
                copy(name, d).wait_send()


def on_device(sizes, right_side, conductivity, guess):
    nx, ny, nz = right_side.shape
    hx = nx // 2
    sweeps = KSWEEP - 1
    fine = (ny + 8, nz + LANES)
    coarse = (ny + 16, nz + LANES)
    rows_a = 2 * nx + hx
    rows_d = (FINE - 1) * nx + (COARSE - 1) * hx
    rows_b = FINE * nx + COARSE * hx
    vmem = lambda *shape: pltpu.VMEM(shape, jnp.float32)
    block = jax.ShapeDtypeStruct((nx, ny, nz), jnp.float32)
    anywhere = pl.BlockSpec(memory_space=pl.ANY)
    inside = pl.BlockSpec(memory_space=pltpu.VMEM)
    messages = 2 + 4 + 2 + 4 + 4 + 4 + 2 + 4 + 2 * sweeps
    both = pl.pallas_call(
        functools.partial(kernel, sizes),
        out_shape=jax.ShapeDtypeStruct((2, nx, ny, nz), jnp.float32),
        in_specs=[anywhere] * 3,
        out_specs=inside,
        scratch_shapes=[
            *[vmem(nx, ny, nz)] * 3,
            vmem(hx, ny, nz),
            vmem(nx, ny, nz),
            vmem(hx, ny, nz),
            *[vmem(2, 3, ny, nz)] * 2,
            *[vmem(2, rows_a, nz)] * 2,
            *[vmem(2, rows_d, nz)] * 2,
            *[vmem(2, ny, LANES)] * 2,
            vmem(4, 8, LANES),
            *[vmem(2, rows_b, nz)] * 2,
            *[vmem(2, ny, LANES)] * 2,
            vmem(4, 8, LANES),
            *[vmem(2, fine[0] + coarse[0], fine[1])] * 2,
            *[vmem(2, 2, *fine)] * 2,
            *[vmem(sweeps, 2, *coarse)] * 2,
            pltpu.SemaphoreType.DMA((3,)),
            pltpu.SemaphoreType.DMA((messages,)),
            pltpu.SemaphoreType.DMA((messages,)),
        ],
        compiler_params=pltpu.CompilerParams(
            collective_id=0, has_side_effects=True, vmem_limit_bytes=60 * 1024 * 1024
        ),
        cost_estimate=pl.CostEstimate(
            flops=300 * nx * ny * nz, bytes_accessed=20 * nx * ny * nz, transcendentals=0
        ),
    )(right_side, conductivity, guess)
    return both[0], both[1]


def solution(mesh):
    spec = P("pencil", "coarse", "gz")
    return jax.shard_map(
        functools.partial(on_device, tuple(mesh.shape[a] for a in AXES)),
        mesh=mesh,
        in_specs=(spec, spec, spec),
        out_specs=(spec, spec),
        check_vma=False,
    )
```
